32 devices in a mesh: group: 2 (over x), expert: 8 (over z, y), attn: 2 (over core).
Axes of the slice: x: 2, y: 2, z: 4, core: 2. Of those that a mesh axis runs over, the one named last changes fastest.
Arguments:
- tokens: bfloat16 [4096, 7168], P(('group', 'expert', 'attn')), parts along dimension 0, may hold values from -6 to 6
- expert_ids: int32 [4096, 4], P(('group', 'expert', 'attn')), parts along dimension 0, may hold values from 0 to 7, all different within a row; in each aligned block of 128 rows (0 to 127, 128 to 255, ...) at most 80 rows name the same one
- gate_values: float32 [4096, 4], P(('group', 'expert', 'attn')), parts along dimension 0, may hold values from 0.1 to 1
- w_gate: bfloat16 [8, 7168, 1024], P('expert', None, 'attn'), may hold values from -0.0625 to 0.0625
- w_up: bfloat16 [8, 7168, 1024], P('expert', None, 'attn'), may hold values from -0.0625 to 0.0625
- w_down: bfloat16 [8, 1024, 7168], P('expert', 'attn'), may hold values from -0.1875 to 0.1875
Outputs:
- mixed_out: bfloat16 [4096, 7168], P(('group', 'expert', 'attn')), parts along dimension 0
The draws below stay inside these ranges and needn't reach their ends.
There are 2 independent parts, one for each index of `group`. The reference program is written for one: setup_inputs(seed, part) draws one part's arguments, and reference() takes and returns one part's arrays. A program takes and returns all parts, laid end to end along the dimension named above; an argument that names none is the same for every part. Nothing has to cross between parts.
Inputs may be any that keep to these rules, and one draw needn't show every extreme that they name: `expert_ids`: each row names 4 different experts. Within the rows of one device no expert is named more than 80 times, a bound that some block reaches.
All inputs are finite; a program needn't handle non-finite values.
Results may differ from the reference program's by a relative error of at most 0.0065.
Values may be sent and summed in bfloat16 or wider, within the bound.
A program may use at most 128 MiB of HBM per device.

```python
import math
import jax
import jax.numpy as jnp
import numpy as np
from jax import lax

D = 7168
FF = 1024
TOP = 4
TOK_DEV = 128
EXPERTS = 8
CAP = 80
TOKENS = 2048
N_ATTN = 2


def block_scale(stream_key, extent, cuts, least, top_value):
    factor_of, own = 1.0, jax.random.fold_in(stream_key, 6)
    for dim, shards_of in cuts:
        heights = jnp.exp(jax.random.uniform(jax.random.fold_in(own, dim), (shards_of,), jnp.float32, least / len(cuts), top_value / len(cuts)))
        factor_of = factor_of * jnp.repeat(heights, extent[dim] // shards_of).reshape([-1 if axis == dim else 1 for axis in range(len(extent))])
    return factor_of


def routed_block(rng, own, number, rows, count, top, reach, lean):
    sequence = jax.random.permutation(rng, count)
    crowded, common = shares(count, rows * top, reach, lean, True), shares(count, rows * top, reach, lean, False)
    places = jnp.arange(count)

    def named(sizes, turn):
        used = int((sizes > 0).sum())
        fixed = max(1, used // 4)
        shifted = fixed + (places - fixed + turn * (used - fixed)) % max(1, count - fixed)
        return jnp.zeros((count,), jnp.int32).at[sequence[jnp.where(places < fixed, places, shifted)]].set(jnp.asarray(sizes, jnp.int32))

    sizes = jnp.where(number % 4 == 0, named(crowded, number // 4), named(common, number - number // 4 - 1))
    mixed = jax.random.permutation(jax.random.fold_in(own, 3), count)
    donor, receiver = mixed[0:count // 2 * 2:2], mixed[1:count // 2 * 2:2]
    room = jnp.minimum(sizes[donor] - 1, reach - sizes[receiver]) // 2
    room = jnp.where((donor == sequence[0]) | (receiver == sequence[0]) | (sizes[receiver] == 0), 0, jnp.maximum(room, 0))
    shifted = jax.random.randint(jax.random.fold_in(own, 4), (count // 2,), 0, 1 << 20) % (room + 1)
    sizes = sizes.at[donor].add(-shifted).at[receiver].add(shifted)
    members = jnp.searchsorted(jnp.cumsum(sizes), jnp.arange(rows * top), side="right").astype(jnp.int32)
    table = members.reshape(top, rows).T
    table = table[jax.random.permutation(jax.random.fold_in(own, 1), rows)]
    turn = jax.random.randint(jax.random.fold_in(own, 2), (rows, 1), 0, top)
    return jnp.take_along_axis(table, (jnp.arange(top)[None, :] + turn) % top, axis=1)


def shares(amount, total, reach, slope, full):
    portions = [(1 << 20) // math.isqrt(standing ** slope) + 1 for standing in range(1, amount + 1)]
    largest = reach if full else min(reach, max(-(-total // amount), total * portions[0] // sum(portions)))
    least = 1 if total - largest >= amount - 1 else 0
    given, rest = [largest] + [least] * (amount - 1), total - largest - least * (amount - 1)
    while rest > 0:
        free = [i for i in range(1, amount) if given[i] < largest] or [i for i in range(1, amount) if given[i] < reach]
        whole, remaining = sum([portions[i] for i in free]), rest
        for i in free:
            extra = min(reach - given[i], max(1, remaining * portions[i] // whole), rest)
            given[i] = given[i] + extra
            rest = rest - extra
    return np.array(given)


def gaussian(stream_key, extent, deviation, bound, cuts=(), held_as=jnp.bfloat16):
    entries = deviation * jax.random.normal(stream_key, extent, jnp.float32)
    if cuts:
        entries = entries * block_scale(stream_key, extent, cuts, -0.22, 0.18)
    return jnp.clip(entries, -bound, bound).astype(held_as)


def setup_inputs(seed: int = 0, part: int = 0) -> dict:
    key_list = jax.random.split(jax.random.key(seed), 7)
    own_keys = jax.random.split(jax.random.fold_in(key_list[6], part), 7)
    tokens = gaussian(own_keys[0], (TOKENS, D), 1.0, 6.0, ((0, 16),))
    expert_ids_keys = jax.random.split(jax.random.fold_in(own_keys[1], 1), TOKENS // TOK_DEV)
    expert_ids_turns = jax.random.permutation(jax.random.fold_in(own_keys[1], 3), TOKENS // TOK_DEV)
    expert_ids = jax.vmap(lambda own, number: routed_block(jax.random.fold_in(own_keys[1], 2), own, number, TOK_DEV, EXPERTS, TOP, CAP, 2))(expert_ids_keys, expert_ids_turns).reshape((TOKENS, TOP))
    gate_values = jnp.clip(0.1 + 0.9 * jax.random.uniform(own_keys[2], (TOKENS, TOP), jnp.float32) ** block_scale(own_keys[2], (TOKENS, TOP), ((0, 16),), -0.2, 0.2), 0.1, 1.0)
    w_gate = gaussian(key_list[3], (EXPERTS, D, FF), D ** -0.5, 0.0625, ((0, 8), (2, 2)))
    w_up = gaussian(key_list[4], (EXPERTS, D, FF), D ** -0.5, 0.0625, ((0, 8), (2, 2)))
    w_down = gaussian(key_list[5], (EXPERTS, FF, D), FF ** -0.5, 0.1875, ((0, 8), (1, 2)))
    return {"tokens": tokens, "expert_ids": expert_ids, "gate_values": gate_values, "w_gate": w_gate, "w_up": w_up, "w_down": w_down}


def reference(tokens, expert_ids, gate_values, w_gate, w_up, w_down):
    blocks = TOKENS // TOK_DEV
    flat_ids = expert_ids.reshape(blocks, TOK_DEV * TOP)
    onehot = (flat_ids[:, :, None] == jnp.arange(EXPERTS, dtype=jnp.int32)[None, None, :]).astype(jnp.int32)
    before = jnp.cumsum(onehot, axis=1) - onehot
    slot_index = jnp.sum(before * onehot, axis=2).reshape(TOKENS, TOP).astype(jnp.int32)
    block_of = (jnp.arange(TOKENS, dtype=jnp.int32) // TOK_DEV).astype(jnp.int32)
    block_two = jnp.broadcast_to(block_of[:, None], (TOKENS, TOP))
    rows_src = jnp.broadcast_to(jnp.arange(TOKENS, dtype=jnp.int32)[:, None], (TOKENS, TOP))
    buffer = jnp.zeros((EXPERTS, blocks, CAP, D), jnp.bfloat16)
    buffer = buffer.at[expert_ids, block_two, slot_index].set(tokens[rows_src])
    half_width = FF // N_ATTN

    def expert_run(packed):
        expert_rows, gate_proj, up_proj, down_proj = packed
        flat_rows = expert_rows.reshape(blocks * CAP, D)
        accum_sum = jnp.zeros((blocks * CAP, D), jnp.float32)
        for core_index in range(N_ATTN):
            lower = core_index * half_width
            gate_act = jnp.dot(flat_rows, gate_proj[:, lower:lower + half_width], preferred_element_type=jnp.float32)
            up_act = jnp.dot(flat_rows, up_proj[:, lower:lower + half_width], preferred_element_type=jnp.float32)
            hidden = (jax.nn.silu(gate_act) * up_act).astype(jnp.bfloat16)
            partial_value = jnp.dot(hidden, down_proj[lower:lower + half_width, :], preferred_element_type=jnp.float32).astype(jnp.bfloat16)
            accum_sum = accum_sum + partial_value.astype(jnp.float32)
        return accum_sum.astype(jnp.bfloat16).reshape(blocks, CAP, D)

    expert_out = lax.map(expert_run, (buffer, w_gate, w_up, w_down))
    picked = expert_out[expert_ids, block_two, slot_index]
    mixed_out = jnp.sum(picked.astype(jnp.float32) * gate_values[:, :, None], axis=1)
    return mixed_out.astype(jnp.bfloat16)
```

```python
import jax
import jax.numpy as jnp
from jax import lax
from jax.sharding import PartitionSpec as P


def shards(tokens, expert_ids, gate_values, w_gate, w_up, w_down):
    experts = lax.axis_size("expert")
    chosen = expert_ids[:, :, None] == jnp.arange(experts, dtype=jnp.int32)[None, None, :]
    weight = jnp.sum(jnp.where(chosen, gate_values[:, :, None], 0.0), axis=1)
    weights = lax.all_gather(weight, ("expert", "attn"), axis=0, tiled=True)
    mine = lax.dynamic_index_in_dim(weights, lax.axis_index("expert"), 1, keepdims=True)
    rows = lax.all_gather(tokens, ("expert", "attn"), axis=0, tiled=True)
    gate_act = jnp.dot(rows, w_gate[0], preferred_element_type=jnp.float32)
    up_act = jnp.dot(rows, w_up[0], preferred_element_type=jnp.float32)
    hidden = (jax.nn.silu(gate_act) * up_act * mine).astype(jnp.bfloat16)
    partial_value = jnp.dot(hidden, w_down[0], preferred_element_type=jnp.float32).astype(jnp.bfloat16)
    return lax.psum_scatter(partial_value, ("expert", "attn"), scatter_dimension=0, tiled=True)


def solution(mesh):
    placed = (
        P(("group", "expert", "attn"), None),
        P(("group", "expert", "attn"), None),
        P(("group", "expert", "attn"), None),
        P("expert", None, "attn"),
        P("expert", None, "attn"),
        P("expert", "attn", None),
    )
    return jax.shard_map(
        shards,
        mesh=mesh,
        in_specs=placed,
        out_specs=P(("group", "expert", "attn"), None),
        check_vma=False,
    )
```

```python
import functools
import jax
import jax.numpy as jnp
from jax import lax
from jax.experimental import pallas as pl
from jax.experimental.pallas import tpu as pltpu
from jax.sharding import PartitionSpec as P

MESH = pl.DeviceIdType.MESH
SUBS = 2
TILE = 256


def ring_kernel(experts, x_ref, wt_ref, wg_ref, wu_ref, wd_ref, out_ref, sib_ref,
                gates, ups, own, held, far, own_wt, held_wt, far_wt,
                hid_own, hid, hid_far, first_out, first_in, second_out,
                load_sem, sib_send, sib_recv, ag_send, ag_recv, wt_send, wt_recv,
                far_send, far_recv, rs_send, rs_recv, down_sem):
    half = experts // 2
    rows, width = x_ref.shape
    units = wg_ref.shape[1]
    part = width // SUBS
    mid = rows // 2
    me = lax.axis_index("expert")
    core = lax.axis_index("attn")

    def owner_at(pos):
        turn = pos // half
        line = pos + turn * (experts - 1 - 2 * pos)
        return 2 * line + turn

    line, turn = me // 2, me % 2
    pos = line + turn * (experts - 1 - 2 * line)
    right = {"expert": owner_at((pos + 1) % experts)}
    left = {"expert": owner_at((pos + experts - 1) % experts)}
    other = {"attn": 1 - core}

    barrier = pltpu.get_barrier_semaphore()
    for peer in (left, right, other):
        pl.semaphore_signal(barrier, inc=1, device_id=peer, device_id_type=MESH)
    pl.semaphore_wait(barrier, 3)

    def remote(src, dst, send, recv, peer):
        return pltpu.make_async_remote_copy(
            src_ref=src, dst_ref=dst, send_sem=send, recv_sem=recv,
            device_id=peer, device_id_type=MESH)

    def side_rows(side):
        return pl.ds(side * rows, rows)

    def gather_copies(dist):
        copies = []
        for side, peer in ((0, right), (1, left)):
            for j in range(SUBS):
                if dist == 1:
                    src = x_ref.at[:, pl.ds(j * part, part)]
                else:
                    src = held.at[dist - 2, j, side_rows(side)]
                copies.append(remote(src, held.at[dist - 1, j, side_rows(side)],
                                     ag_send.at[dist - 1, side, j], ag_recv.at[dist - 1, side, j], peer))
            wsrc = wt_ref if dist == 1 else held_wt.at[dist - 2, side]
            copies.append(remote(wsrc, held_wt.at[dist - 1, side],
                                 wt_send.at[dist - 1, side], wt_recv.at[dist - 1, side], peer))
        return copies

    def far_copies():
        copies = []
        for side, peer in ((0, right), (1, left)):
            for j in range(SUBS):
                copies.append(remote(held.at[half - 2, j, pl.ds(side * rows + side * mid, mid)],
                                     far.at[j, pl.ds(side * mid, mid)],
                                     far_send.at[side, j], far_recv.at[side, j], peer))
        copies.append(remote(held_wt.at[half - 2, 0], far_wt, wt_send.at[half - 1, 0],
                             wt_recv.at[half - 1, 0], right))
        return copies

    hops = [gather_copies(dist) for dist in range(1, half)] + [far_copies()]
    for copy in hops[0]:
        copy.start()

    loads = [pltpu.make_async_copy(wg_ref, gates.at[core], load_sem.at[0]),
             pltpu.make_async_copy(wu_ref, ups.at[core], load_sem.at[1]),
             pltpu.make_async_copy(wt_ref, own_wt, load_sem.at[2])]
    for j in range(SUBS):
        loads.append(pltpu.make_async_copy(x_ref.at[:, pl.ds(j * part, part)], own.at[j], load_sem.at[3 + j]))
    swaps = [remote(wg_ref, gates.at[core], sib_send.at[0], sib_recv.at[0], other),
             remote(wu_ref, ups.at[core], sib_send.at[1], sib_recv.at[1], other),
             remote(wd_ref, sib_ref, sib_send.at[2], sib_recv.at[2], other)]
    for copy in loads + swaps:
        copy.start()

    def column(table):
        names = lax.broadcasted_iota(jnp.int32, table.shape, 0)
        line_of = jnp.sum(jnp.where(names == me, table, 0.0), axis=0, keepdims=True)
        square = (rows, rows)
        same = lax.broadcasted_iota(jnp.int32, square, 0) == lax.broadcasted_iota(jnp.int32, square, 1)
        return jnp.sum(jnp.where(same, jnp.broadcast_to(line_of, square), 0.0), axis=1, keepdims=True)

    def expand(chunks, weight, target):
        def one(q, carry):
            r, n = q // (units // TILE), q % (units // TILE)
            cols = pl.ds(pl.multiple_of(n * TILE, TILE), TILE)
            gate_act = jnp.zeros((weight.shape[0], TILE), jnp.float32)
            up_act = gate_act
            for j, chunk in enumerate(chunks):
                deep = pl.ds(j * part, part)
                gate_act += jnp.dot(chunk[...], gates[r, deep, cols], preferred_element_type=jnp.float32)
                up_act += jnp.dot(chunk[...], ups[r, deep, cols], preferred_element_type=jnp.float32)
            value = gate_act / (1.0 + jnp.exp(-gate_act)) * up_act * weight
            target[:, pl.ds(pl.multiple_of(q * TILE, TILE), TILE)] = value.astype(jnp.bfloat16)
            return carry

        lax.fori_loop(0, 2 * units // TILE, one, 0)

    for dist in range(1, half):
        for copy in hops[dist - 1]:
            copy.wait_recv()
        for copy in hops[dist]:
            copy.start()
        if dist == 1:
            for copy in loads:
                copy.wait()
            for copy in swaps[:2]:
                copy.wait()
            expand([own.at[j] for j in range(SUBS)], column(own_wt[...]), hid_own)
        weight = jnp.concatenate([column(held_wt[dist - 1, 0]), column(held_wt[dist - 1, 1])], axis=0)
        expand([held.at[dist - 1, j] for j in range(SUBS)], weight, hid.at[dist - 1])
    swaps[2].wait()
    for copy in hops[half - 1]:
        copy.wait_recv()
    expand([far.at[j] for j in range(SUBS)], column(far_wt[...]), hid_far)
    for hop in hops:
        for copy in hop:
            copy.wait_send()

    blocks = width // units

    def down_copy(r, b):
        place = pl.ds(pl.multiple_of(b * units, units), units)
        return [pltpu.make_async_copy(wd_ref.at[:, place], gates.at[core, place], down_sem.at[0, b]),
                pltpu.make_async_copy(sib_ref.at[:, place], gates.at[1 - core, place], down_sem.at[1, b])]

    def start_down(b, carry):
        for copy in down_copy(0, b):
            copy.start()
        return carry

    def wait_down(b, carry):
        for copy in down_copy(0, b):
            copy.wait()
        return carry

    lax.fori_loop(0, blocks, start_down, 0)
    lax.fori_loop(0, blocks, wait_down, 0)

    def contract(j, hidden, write):
        def one(t, carry):
            place = pl.ds(pl.multiple_of((j * (part // units) + t) * units, units), units)
            total = jnp.dot(hidden[:, :units], gates[0, place, :], preferred_element_type=jnp.float32)
            total += jnp.dot(hidden[:, units:], gates[1, place, :], preferred_element_type=jnp.float32)
            write(pl.ds(pl.multiple_of(t * units, units), units), total)
            return carry

        lax.fori_loop(0, part // units, one, 0)

    sums = {}
    for j in range(SUBS):
        def write(cols, total, j=j):
            first_out[j, :, cols] = total.astype(jnp.bfloat16)

        contract(j, hid_far, write)
        pair = []
        for side, peer in ((0, left), (1, right)):
            piece = pl.ds((1 - side) * mid, mid)
            pair.append(remote(first_out.at[j, piece], first_in.at[j, piece],
                               rs_send.at[0, side, j], rs_recv.at[0, side, j], peer))
        for copy in pair:
            copy.start()
        sums[0, j] = pair
    for k in range(1, half):
        dist = half - k
        for j in range(SUBS):
            for copy in sums[k - 1, j]:
                copy.wait_recv()
            if k == 1:
                source = second_out.at[j]

                def write(cols, total, j=j):
                    second_out[j, :mid, cols] = total[:mid].astype(jnp.bfloat16)
                    second_out[j, mid:rows, cols] = (
                        total[mid:rows] + first_in[j, mid:, cols].astype(jnp.float32)).astype(jnp.bfloat16)
                    second_out[j, rows:rows + mid, cols] = (
                        total[rows:rows + mid] + first_in[j, :mid, cols].astype(jnp.float32)).astype(jnp.bfloat16)
                    second_out[j, rows + mid:, cols] = total[rows + mid:].astype(jnp.bfloat16)
            else:
                source = held.at[k - 2, j]

                def write(cols, total, k=k, j=j):
                    held[k - 2, j, :, cols] = (
                        total + held[k - 2, j, :, cols].astype(jnp.float32)).astype(jnp.bfloat16)

            contract(j, hid.at[dist - 1], write)
            pair = []
            for side, peer in ((0, left), (1, right)):
                pair.append(remote(source.at[side_rows(side)], held.at[k - 1, j, side_rows(side)],
                                   rs_send.at[k, side, j], rs_recv.at[k, side, j], peer))
            for copy in pair:
                copy.start()
            sums[k, j] = pair
    for j in range(SUBS):
        for copy in sums[half - 1, j]:
            copy.wait_recv()

        def write(cols, total, j=j):
            both = held[half - 2, j, :rows, cols].astype(jnp.float32) + held[half - 2, j, rows:, cols].astype(jnp.float32)
            own[j, :, cols] = (total + both).astype(jnp.bfloat16)

        contract(j, hid_own, write)
        out_ref[:, j * part:(j + 1) * part] = own[j]
    for pair in sums.values():
        for copy in pair:
            copy.wait_send()


def ring_shards(tokens, expert_ids, gate_values, w_gate, w_up, w_down):
    experts = lax.axis_size("expert")
    rows, width = tokens.shape
    units = w_gate.shape[2]
    half = experts // 2
    chosen = expert_ids.T[:, None, :] == jnp.arange(experts, dtype=jnp.int32)[None, :, None]
    table = jnp.sum(jnp.where(chosen, gate_values.T[:, None, :], 0.0), axis=0)
    part = width // SUBS
    bf, f32 = jnp.bfloat16, jnp.float32
    dma = pltpu.SemaphoreType.DMA
    anywhere = pl.BlockSpec(memory_space=pl.ANY)
    out, _ = pl.pallas_call(
        functools.partial(ring_kernel, experts),
        out_shape=(jax.ShapeDtypeStruct((rows, width), bf), jax.ShapeDtypeStruct((units, width), bf)),
        in_specs=[anywhere] * 5,
        out_specs=(pl.BlockSpec(memory_space=pltpu.VMEM), anywhere),
        scratch_shapes=[
            pltpu.VMEM((2, width, units), bf),
            pltpu.VMEM((2, width, units), bf),
            pltpu.VMEM((SUBS, rows, part), bf),
            pltpu.VMEM((half - 1, SUBS, 2 * rows, part), bf),
            pltpu.VMEM((SUBS, rows, part), bf),
            pltpu.VMEM((experts, rows), f32),
            pltpu.VMEM((half - 1, 2, experts, rows), f32),
            pltpu.VMEM((experts, rows), f32),
            pltpu.VMEM((rows, 2 * units), bf),
            pltpu.VMEM((half - 1, 2 * rows, 2 * units), bf),
            pltpu.VMEM((rows, 2 * units), bf),
            pltpu.VMEM((SUBS, rows, part), bf),
            pltpu.VMEM((SUBS, rows, part), bf),
            pltpu.VMEM((SUBS, 2 * rows, part), bf),
            dma((3 + SUBS,)), dma((3,)), dma((3,)),
            dma((half - 1, 2, SUBS)), dma((half - 1, 2, SUBS)),
            dma((half, 2)), dma((half, 2)),
            dma((2, SUBS)), dma((2, SUBS)),
            dma((half, 2, SUBS)), dma((half, 2, SUBS)),
            dma((2, width // units)),
        ],
        compiler_params=pltpu.CompilerParams(
            collective_id=0, has_side_effects=True, vmem_limit_bytes=60 * 2 ** 20),
    )(tokens, table, w_gate[0], w_up[0], w_down[0])
    return out


def shards(tokens, expert_ids, gate_values, w_gate, w_up, w_down):
    experts = lax.axis_size("expert")
    tok_rows = tokens.shape[0]
    top_count = expert_ids.shape[1]
    width = tokens.shape[1]
    capacity = (tok_rows * top_count * 5 // (4 * experts) + 7) // 8 * 8
    flat_ids = expert_ids.reshape(-1)
    onehot = (flat_ids[:, None] == jnp.arange(experts, dtype=jnp.int32)[None, :]).astype(jnp.int32)
    before = jnp.cumsum(onehot, axis=0) - onehot
    slot_index = jnp.sum(before * onehot, axis=1)
    position = flat_ids * capacity + slot_index
    placing = jnp.arange(experts * capacity, dtype=jnp.int32)[:, None] == position[None, :]
    placing = jnp.sum(
        placing.reshape(experts * capacity, tok_rows, top_count).astype(jnp.int32), axis=2
    ).astype(jnp.bfloat16)
    outgoing = jnp.dot(placing, tokens, preferred_element_type=jnp.float32).astype(jnp.bfloat16)
    outgoing = outgoing.reshape(experts, capacity, width)
    gate_proj = w_gate[0]
    up_proj = w_up[0]
    down_proj = w_down[0]
    paired = lax.all_gather(
        lax.all_to_all(outgoing, "expert", split_axis=0, concat_axis=0, tiled=True),
        "attn",
        axis=1,
        tiled=True,
    )
    flat_rows = paired.reshape(-1, width)
    gate_act = jnp.dot(flat_rows, gate_proj, preferred_element_type=jnp.float32)
    up_act = jnp.dot(flat_rows, up_proj, preferred_element_type=jnp.float32)
    hidden = (jax.nn.silu(gate_act) * up_act).astype(jnp.bfloat16)
    partial_value = (
        jnp.dot(hidden, down_proj, preferred_element_type=jnp.float32)
        .astype(jnp.bfloat16)
        .reshape(paired.shape)
    )
    summed = (
        lax.psum_scatter(partial_value, "attn", scatter_dimension=1, tiled=True)
        .astype(jnp.float32)
        .astype(jnp.bfloat16)
    )
    returned = lax.all_to_all(summed, "expert", split_axis=0, concat_axis=0, tiled=True)
    picked = returned.reshape(experts * capacity, width)[position]
    picked = picked.reshape(tok_rows, top_count, width)
    mixed_out = jnp.sum(picked.astype(jnp.float32) * gate_values[:, :, None], axis=1)
    return mixed_out.astype(jnp.bfloat16)


def solution(mesh):
    placed = (
        P(("group", "expert", "attn"), None),
        P(("group", "expert", "attn"), None),
        P(("group", "expert", "attn"), None),
        P("expert", None, "attn"),
        P("expert", None, "attn"),
        P("expert", "attn", None),
    )

    def run(tokens, expert_ids, gate_values, w_gate, w_up, w_down):
        experts, cores = mesh.shape["expert"], mesh.shape["attn"]
        block = tokens.size * 2 // mesh.size
        weights = w_gate.size * 2 // experts
        need = block * (experts + 7) + 2 * weights
        fits = cores == 2 and experts % 2 == 0 and experts >= 4 and need <= 58 * 2 ** 20
        return jax.shard_map(
            ring_shards if fits else shards,
            mesh=mesh,
            in_specs=placed,
            out_specs=P(("group", "expert", "attn"), None),
            check_vma=False,
        )(tokens, expert_ids, gate_values, w_gate, w_up, w_down)

    return run
```

```python
import functools
import jax
import jax.numpy as jnp
from jax import lax
from jax.experimental import pallas as pl
from jax.experimental.pallas import tpu as pltpu
from jax.sharding import PartitionSpec as P

MESH = pl.DeviceIdType.MESH
SUBS = 2
TILE = 256


def ring_kernel(experts, x_ref, wt_ref, wg_ref, wu_ref, wd_ref, out_ref, sib_ref,
                gates, ups, own, held, late, far, own_wt, held_wt, far_wt,
                hid_own, hid, hid_late, hid_far, hid_wide, stage, stage_far, first_in, late_in, second_out,
                load_sem, sib_send, sib_recv, ag_send, ag_recv, wt_send, wt_recv,
                rs_send, rs_recv, down_sem):
    half = experts // 2
    rows, width = x_ref.shape
    units = wg_ref.shape[1]
    part = width // SUBS
    cap = far.shape[1]
    me = lax.axis_index("expert")
    core = lax.axis_index("attn")

    def owner_at(pos):
        turn = pos // half
        line = pos + turn * (experts - 1 - 2 * pos)
        return 2 * line + turn

    line, turn = me // 2, me % 2
    pos = line + turn * (experts - 1 - 2 * line)
    right_owner = owner_at((pos + 1) % experts)
    left_owner = owner_at((pos + experts - 1) % experts)
    right, left = {"expert": right_owner}, {"expert": left_owner}
    other = {"attn": 1 - core}

    barrier = pltpu.get_barrier_semaphore()
    for peer in (left, right, other):
        pl.semaphore_signal(barrier, inc=1, device_id=peer, device_id_type=MESH)
    pl.semaphore_wait(barrier, 3)

    def remote(src, dst, send, recv, peer):
        return pltpu.make_async_remote_copy(
            src_ref=src, dst_ref=dst, send_sem=send, recv_sem=recv,
            device_id=peer, device_id_type=MESH)

    ahead = ((right, right_owner), (left, left_owner))

    def side_rows(side):
        return pl.ds(side * rows, rows)

    def cap_rows(side):
        return pl.ds(side * cap, cap)

    def hop_copy(dist, side, j):
        if dist == half:
            src, dst = stage_far.at[side], far.at[j]
        elif dist == half - 1 and j != side:
            src, dst = stage.at[side], late.at[j, cap_rows(side)]
        else:
            src = x_ref.at[:, pl.ds(j * part, part)] if dist == 1 else held.at[dist - 2, j, side_rows(side)]
            dst = held.at[dist - 1, j, side_rows(side)]
        return remote(src, dst, ag_send.at[dist - 1, side, j], ag_recv.at[dist - 1, side, j], ahead[side][0])

    def table_copy(dist, side):
        src = wt_ref if dist == 1 else held_wt.at[dist - 2, side]
        dst = far_wt if dist == half else held_wt.at[dist - 1, side]
        return remote(src, dst, wt_send.at[dist - 1, side], wt_recv.at[dist - 1, side], ahead[side][0])

    hops, tables = {}, {}
    for dist in range(1, half + 1):
        for side in range(2):
            if dist < half or side == 0:
                tables[dist, side] = table_copy(dist, side)
            for j in range(SUBS):
                if dist < half or j == side:
                    hops[dist, side, j] = hop_copy(dist, side, j)
    for side in range(2):
        tables[1, side].start()
    for j in range(SUBS):
        for side in range(2):
            hops[1, side, j].start()

    loads = [pltpu.make_async_copy(wg_ref, gates.at[core], load_sem.at[0]),
             pltpu.make_async_copy(wu_ref, ups.at[core], load_sem.at[1]),
             pltpu.make_async_copy(wt_ref, own_wt, load_sem.at[2])]
    for j in range(SUBS):
        loads.append(pltpu.make_async_copy(x_ref.at[:, pl.ds(j * part, part)], own.at[j], load_sem.at[3 + j]))
    swaps = [remote(wg_ref, gates.at[core], sib_send.at[0], sib_recv.at[0], other),
             remote(wu_ref, ups.at[core], sib_send.at[1], sib_recv.at[1], other),
             remote(wd_ref, sib_ref, sib_send.at[2], sib_recv.at[2], other)]
    for copy in loads + swaps:
        copy.start()

    def line_of(table, name):
        names = lax.broadcasted_iota(jnp.int32, table.shape, 0)
        return jnp.sum(jnp.where(names == name, table, 0.0), axis=0, keepdims=True)

    def column(flat):
        square = (rows, rows)
        same = lax.broadcasted_iota(jnp.int32, square, 0) == lax.broadcasted_iota(jnp.int32, square, 1)
        return jnp.sum(jnp.where(same, jnp.broadcast_to(flat, square), 0.0), axis=1, keepdims=True)

    def chosen_rows(table, owner):
        slots = jnp.broadcast_to(line_of(table, experts + owner), (cap, rows)).astype(jnp.int32)
        return slots == lax.broadcasted_iota(jnp.int32, (cap, rows), 0)

    def ones(mask):
        return jnp.where(mask, 1.0, 0.0).astype(jnp.bfloat16)

    def spread(table, owner):
        slots = jnp.broadcast_to(column(line_of(table, experts + owner)), (rows, cap)).astype(jnp.int32)
        return ones(slots == lax.broadcasted_iota(jnp.int32, (rows, cap), 1))

    def narrow(mask, source, target):
        def one(t, carry):
            cols = pl.ds(pl.multiple_of(t * units, units), units)
            target[:, cols] = jnp.dot(mask, source[:, cols], preferred_element_type=jnp.float32).astype(jnp.bfloat16)
            return carry

        lax.fori_loop(0, part // units, one, 0)

    def narrow_weight(table):
        picked = chosen_rows(table, me)
        return jnp.sum(jnp.where(picked, jnp.broadcast_to(line_of(table, me), (cap, rows)), 0.0), axis=1, keepdims=True)

    def expand(chunks, weight, target):
        def one(q, carry):
            r, n = q // (units // TILE), q % (units // TILE)
            cols = pl.ds(pl.multiple_of(n * TILE, TILE), TILE)
            gate_act = jnp.zeros((weight.shape[0], TILE), jnp.float32)
            up_act = gate_act
            for j, chunk in enumerate(chunks):
                deep = pl.ds(j * part, part)
                gate_act += jnp.dot(chunk[...], gates[r, deep, cols], preferred_element_type=jnp.float32)
                up_act += jnp.dot(chunk[...], ups[r, deep, cols], preferred_element_type=jnp.float32)
            value = gate_act / (1.0 + jnp.exp(-gate_act)) * up_act * weight
            target[:, pl.ds(pl.multiple_of(q * TILE, TILE), TILE)] = value.astype(jnp.bfloat16)
            return carry

        lax.fori_loop(0, 2 * units // TILE, one, 0)

    for dist in range(1, half):
        for side in range(2):
            tables[dist, side].wait_recv()
            if (dist + 1, side) in tables:
                tables[dist + 1, side].start()
        if dist == half - 1:
            for side in range(2):
                for j in range(SUBS):
                    hops[2, side, j].wait_send()
        for j in range(SUBS):
            for side in range(2):
                hops[dist, side, j].wait_recv()
                if (dist + 1, side, j) not in hops:
                    continue
                if dist + 1 == half or (dist + 1 == half - 1 and j != side):
                    mask = ones(chosen_rows(held_wt[dist - 1, side], ahead[side][1]))
                    narrow(mask, held.at[dist - 1, j, side_rows(side)],
                           stage_far.at[side] if dist + 1 == half else stage.at[side])
                hops[dist + 1, side, j].start()
        if dist == 1:
            for copy in loads:
                copy.wait()
            for copy in swaps[:2]:
                copy.wait()
            expand([own.at[j] for j in range(SUBS)], column(line_of(own_wt[...], me)), hid_own)
        if dist < half - 1:
            weight = jnp.concatenate([column(line_of(held_wt[dist - 1, side], me)) for side in range(2)], axis=0)
            expand([held.at[dist - 1, j] for j in range(SUBS)], weight, hid.at[dist - 1])
        else:
            for side in range(2):
                mask = ones(chosen_rows(held_wt[dist - 1, side], me))
                narrow(mask, held.at[dist - 1, side, side_rows(side)], late.at[side, cap_rows(side)])
            weight = jnp.concatenate([narrow_weight(held_wt[dist - 1, side]) for side in range(2)], axis=0)
            expand([late.at[j] for j in range(SUBS)], weight, hid_late)
    swaps[2].wait()
    tables[half, 0].wait_recv()
    for side in range(2):
        hops[half, side, side].wait_recv()
    expand([far.at[j] for j in range(SUBS)], narrow_weight(far_wt[...]), hid_far)
    for name, copy in hops.items():
        if name[0] != 2:
            copy.wait_send()
    for copy in tables.values():
        copy.wait_send()

    blocks = width // units

    def down_copy(r, b):
        place = pl.ds(pl.multiple_of(b * units, units), units)
        return [pltpu.make_async_copy(wd_ref.at[:, place], gates.at[core, place], down_sem.at[0, b]),
                pltpu.make_async_copy(sib_ref.at[:, place], gates.at[1 - core, place], down_sem.at[1, b])]

    def start_down(b, carry):
        for copy in down_copy(0, b):
            copy.start()
        return carry

    def wait_down(b, carry):
        for copy in down_copy(0, b):
            copy.wait()
        return carry

    lax.fori_loop(0, blocks, start_down, 0)
    lax.fori_loop(0, blocks, wait_down, 0)

    def contract(j, hidden, write):
        def one(t, carry):
            place = pl.ds(pl.multiple_of((j * (part // units) + t) * units, units), units)
            total = jnp.dot(hidden[:, :units], gates[0, place, :], preferred_element_type=jnp.float32)
            total += jnp.dot(hidden[:, units:], gates[1, place, :], preferred_element_type=jnp.float32)
            write(pl.ds(pl.multiple_of(t * units, units), units), total)
            return carry

        lax.fori_loop(0, part // units, one, 0)

    back = ((left, right_owner), (right, left_owner))
    sums = {}

    def send(k, side, j, src, dst):
        copy = remote(src, dst, rs_send.at[k, side, j], rs_recv.at[k, side, j], back[side][0])
        copy.start()
        sums[k, side, j] = copy

    for j in range(SUBS):
        side = 1 - j

        def write(cols, total, side=side):
            stage_far[side, :, cols] = total.astype(jnp.bfloat16)

        contract(j, hid_far, write)
        send(0, side, j, stage_far.at[side], first_in.at[side])
    for j in range(SUBS):
        side = j

        def write(cols, total, side=side):
            stage[side, :, cols] = total.astype(jnp.bfloat16)

        contract(j, hid_late.at[cap_rows(side)], write)
        send(1, side, j, stage.at[side], late_in.at[side])
    for j in range(SUBS):
        side = 1 - j
        table = held_wt[half - 2, side]
        theirs = spread(table, back[side][1])
        hid_own_rows = jnp.dot(spread(table, me), hid_late[cap_rows(side), :], preferred_element_type=jnp.float32)
        hid_wide[...] = hid_own_rows.astype(jnp.bfloat16)
        sums[0, side, j].wait_recv()

        def write(cols, total, side=side, theirs=theirs):
            second_out[side, :, cols] = (
                total + jnp.dot(theirs, first_in[side, :, cols], preferred_element_type=jnp.float32)).astype(jnp.bfloat16)

        contract(j, hid_wide, write)
        send(1, side, j, second_out.at[side], held.at[0, j, side_rows(side)])
    for k in range(2, half):
        dist = half - k
        for j in range(SUBS):
            for side in range(2):
                sums[k - 1, side, j].wait_recv()
            if k == 2:
                theirs = spread(held_wt[dist - 1, j], back[j][1])

                def write(cols, total, j=j, theirs=theirs):
                    early, full = slice(j * rows, (j + 1) * rows), slice((1 - j) * rows, (2 - j) * rows)
                    held[0, j, early, cols] = (total[early] + jnp.dot(
                        theirs, late_in[j, :, cols], preferred_element_type=jnp.float32)).astype(jnp.bfloat16)
                    held[0, j, full, cols] = (
                        total[full] + held[0, j, full, cols].astype(jnp.float32)).astype(jnp.bfloat16)
            else:
                def write(cols, total, k=k, j=j):
                    held[k - 2, j, :, cols] = (
                        total + held[k - 2, j, :, cols].astype(jnp.float32)).astype(jnp.bfloat16)

            contract(j, hid.at[dist - 1], write)
            for side in range(2):
                send(k, side, j, held.at[k - 2, j, side_rows(side)], held.at[k - 1, j, side_rows(side)])
    for j in range(SUBS):
        for side in range(2):
            sums[half - 1, side, j].wait_recv()

        def write(cols, total, j=j):
            both = held[half - 2, j, :rows, cols].astype(jnp.float32) + held[half - 2, j, rows:, cols].astype(jnp.float32)
            own[j, :, cols] = (total + both).astype(jnp.bfloat16)

        contract(j, hid_own, write)
        out_ref[:, j * part:(j + 1) * part] = own[j]
    for copy in sums.values():
        copy.wait_send()


def ring_shards(tokens, expert_ids, gate_values, w_gate, w_up, w_down):
    experts = lax.axis_size("expert")
    rows, width = tokens.shape
    units = w_gate.shape[2]
    half = experts // 2
    chosen = expert_ids.T[:, None, :] == jnp.arange(experts, dtype=jnp.int32)[None, :, None]
    weight = jnp.sum(jnp.where(chosen, gate_values.T[:, None, :], 0.0), axis=0)
    named = jnp.any(chosen, axis=0)
    before = (jnp.arange(rows)[:, None] < jnp.arange(rows)[None, :]).astype(jnp.bfloat16)
    slots = jnp.dot(named.astype(jnp.bfloat16), before, preferred_element_type=jnp.float32)
    table = jnp.concatenate([weight, jnp.where(named, slots, -1.0)], axis=0)
    cap = (rows * expert_ids.shape[1] * 5 // (4 * experts) + 15) // 16 * 16
    part = width // SUBS
    bf, f32 = jnp.bfloat16, jnp.float32
    dma = pltpu.SemaphoreType.DMA
    anywhere = pl.BlockSpec(memory_space=pl.ANY)
    out, _ = pl.pallas_call(
        functools.partial(ring_kernel, experts),
        out_shape=(jax.ShapeDtypeStruct((rows, width), bf), jax.ShapeDtypeStruct((units, width), bf)),
        in_specs=[anywhere] * 5,
        out_specs=(pl.BlockSpec(memory_space=pltpu.VMEM), anywhere),
        scratch_shapes=[
            pltpu.VMEM((2, width, units), bf),
            pltpu.VMEM((2, width, units), bf),
            pltpu.VMEM((SUBS, rows, part), bf),
            pltpu.VMEM((half - 1, SUBS, 2 * rows, part), bf),
            pltpu.VMEM((SUBS, 2 * cap, part), bf),
            pltpu.VMEM((SUBS, cap, part), bf),
            pltpu.VMEM((2 * experts, rows), f32),
            pltpu.VMEM((half - 1, 2, 2 * experts, rows), f32),
            pltpu.VMEM((2 * experts, rows), f32),
            pltpu.VMEM((rows, 2 * units), bf),
            pltpu.VMEM((half - 2, 2 * rows, 2 * units), bf),
            pltpu.VMEM((2 * cap, 2 * units), bf),
            pltpu.VMEM((cap, 2 * units), bf),
            pltpu.VMEM((rows, 2 * units), bf),
            pltpu.VMEM((2, cap, part), bf),
            pltpu.VMEM((2, cap, part), bf),
            pltpu.VMEM((2, cap, part), bf),
            pltpu.VMEM((2, cap, part), bf),
            pltpu.VMEM((2, rows, part), bf),
            dma((3 + SUBS,)), dma((3,)), dma((3,)),
            dma((half, 2, SUBS)), dma((half, 2, SUBS)),
            dma((half, 2)), dma((half, 2)),
            dma((half, 2, SUBS)), dma((half, 2, SUBS)),
            dma((2, width // units)),
        ],
        compiler_params=pltpu.CompilerParams(
            collective_id=0, has_side_effects=True, vmem_limit_bytes=60 * 2 ** 20),
    )(tokens, table, w_gate[0], w_up[0], w_down[0])
    return out


def shards(tokens, expert_ids, gate_values, w_gate, w_up, w_down):
    experts = lax.axis_size("expert")
    tok_rows = tokens.shape[0]
    top_count = expert_ids.shape[1]
    width = tokens.shape[1]
    capacity = (tok_rows * top_count * 5 // (4 * experts) + 7) // 8 * 8
    flat_ids = expert_ids.reshape(-1)
    onehot = (flat_ids[:, None] == jnp.arange(experts, dtype=jnp.int32)[None, :]).astype(jnp.int32)
    before = jnp.cumsum(onehot, axis=0) - onehot
    slot_index = jnp.sum(before * onehot, axis=1)
    position = flat_ids * capacity + slot_index
    placing = jnp.arange(experts * capacity, dtype=jnp.int32)[:, None] == position[None, :]
    placing = jnp.sum(
        placing.reshape(experts * capacity, tok_rows, top_count).astype(jnp.int32), axis=2
    ).astype(jnp.bfloat16)
    outgoing = jnp.dot(placing, tokens, preferred_element_type=jnp.float32).astype(jnp.bfloat16)
    outgoing = outgoing.reshape(experts, capacity, width)
    gate_proj = w_gate[0]
    up_proj = w_up[0]
    down_proj = w_down[0]
    paired = lax.all_gather(
        lax.all_to_all(outgoing, "expert", split_axis=0, concat_axis=0, tiled=True),
        "attn",
        axis=1,
        tiled=True,
    )
    flat_rows = paired.reshape(-1, width)
    gate_act = jnp.dot(flat_rows, gate_proj, preferred_element_type=jnp.float32)
    up_act = jnp.dot(flat_rows, up_proj, preferred_element_type=jnp.float32)
    hidden = (jax.nn.silu(gate_act) * up_act).astype(jnp.bfloat16)
    partial_value = (
        jnp.dot(hidden, down_proj, preferred_element_type=jnp.float32)
        .astype(jnp.bfloat16)
        .reshape(paired.shape)
    )
    summed = (
        lax.psum_scatter(partial_value, "attn", scatter_dimension=1, tiled=True)
        .astype(jnp.float32)
        .astype(jnp.bfloat16)
    )
    returned = lax.all_to_all(summed, "expert", split_axis=0, concat_axis=0, tiled=True)
    picked = returned.reshape(experts * capacity, width)[position]
    picked = picked.reshape(tok_rows, top_count, width)
    mixed_out = jnp.sum(picked.astype(jnp.float32) * gate_values[:, :, None], axis=1)
    return mixed_out.astype(jnp.bfloat16)


def solution(mesh):
    placed = (
        P(("group", "expert", "attn"), None),
        P(("group", "expert", "attn"), None),
        P(("group", "expert", "attn"), None),
        P("expert", None, "attn"),
        P("expert", None, "attn"),
        P("expert", "attn", None),
    )

    def run(tokens, expert_ids, gate_values, w_gate, w_up, w_down):
        experts, cores = mesh.shape["expert"], mesh.shape["attn"]
        block = tokens.size * 2 // mesh.size
        weights = w_gate.size * 2 // experts
        need = block * (experts + 7) + 2 * weights
        fits = cores == 2 and experts % 2 == 0 and experts >= 8 and need <= 58 * 2 ** 20
        return jax.shard_map(
            ring_shards if fits else shards,
            mesh=mesh,
            in_specs=placed,
            out_specs=P(("group", "expert", "attn"), None),
            check_vma=False,
        )(tokens, expert_ids, gate_values, w_gate, w_up, w_down)

    return run
```

```python
import functools
import jax
import jax.numpy as jnp
from jax import lax
from jax.experimental import pallas as pl
from jax.experimental.pallas import tpu as pltpu
from jax.sharding import PartitionSpec as P

MESH = pl.DeviceIdType.MESH
SUBS = 2
TILE = 256


def ring_kernel(experts, x_ref, wt_ref, wg_ref, wu_ref, wd_ref, out_ref, sib_ref,
                gates, ups, own, held, late, far, own_wt, held_wt, far_wt,
                hid_own, hid, hid_late, hid_far, hid_wide, stage, stage_far, first_in, late_in, second_out, tiles,
                load_sem, sib_send, sib_recv, ag_send, ag_recv, wt_send, wt_recv,
                rs_send, rs_recv, down_sem, tile_sem):
    half = experts // 2
    rows, width = x_ref.shape
    units = wg_ref.shape[1]
    part = width // SUBS
    cap = far.shape[1]
    me = lax.axis_index("expert")
    core = lax.axis_index("attn")

    def owner_at(pos):
        turn = pos // half
        line = pos + turn * (experts - 1 - 2 * pos)
        return 2 * line + turn

    line, turn = me // 2, me % 2
    pos = line + turn * (experts - 1 - 2 * line)
    right_owner = owner_at((pos + 1) % experts)
    left_owner = owner_at((pos + experts - 1) % experts)
    right, left = {"expert": right_owner}, {"expert": left_owner}
    other = {"attn": 1 - core}

    barrier = pltpu.get_barrier_semaphore()
    for peer in (left, right, other):
        pl.semaphore_signal(barrier, inc=1, device_id=peer, device_id_type=MESH)
    pl.semaphore_wait(barrier, 3)

    def remote(src, dst, send, recv, peer):
        return pltpu.make_async_remote_copy(
            src_ref=src, dst_ref=dst, send_sem=send, recv_sem=recv,
            device_id=peer, device_id_type=MESH)

    ahead = ((right, right_owner), (left, left_owner))

    def side_rows(side):
        return pl.ds(side * rows, rows)

    def cap_rows(side):
        return pl.ds(side * cap, cap)

    def hop_copy(dist, side, j):
        if dist == half:
            src, dst = stage_far.at[side], far.at[j]
        elif dist == half - 1 and j != side:
            src, dst = stage.at[side], late.at[j, cap_rows(side)]
        else:
            src = x_ref.at[:, pl.ds(j * part, part)] if dist == 1 else held.at[dist - 2, j, side_rows(side)]
            dst = held.at[dist - 1, j, side_rows(side)]
        return remote(src, dst, ag_send.at[dist - 1, side, j], ag_recv.at[dist - 1, side, j], ahead[side][0])

    def table_copy(dist, side):
        src = wt_ref if dist == 1 else held_wt.at[dist - 2, side]
        dst = far_wt if dist == half else held_wt.at[dist - 1, side]
        return remote(src, dst, wt_send.at[dist - 1, side], wt_recv.at[dist - 1, side], ahead[side][0])

    hops, tables = {}, {}
    for dist in range(1, half + 1):
        for side in range(2):
            if dist < half or side == 0:
                tables[dist, side] = table_copy(dist, side)
            for j in range(SUBS):
                if dist < half or j == side:
                    hops[dist, side, j] = hop_copy(dist, side, j)
    for side in range(2):
        tables[1, side].start()
    for j in range(SUBS):
        for side in range(2):
            hops[1, side, j].start()

    loads = [pltpu.make_async_copy(wg_ref, gates.at[core], load_sem.at[0]),
             pltpu.make_async_copy(wu_ref, ups.at[core], load_sem.at[1]),
             pltpu.make_async_copy(wt_ref, own_wt, load_sem.at[2])]
    for j in range(SUBS):
        loads.append(pltpu.make_async_copy(x_ref.at[:, pl.ds(j * part, part)], own.at[j], load_sem.at[3 + j]))
    swaps = [remote(wg_ref, gates.at[core], sib_send.at[0], sib_recv.at[0], other),
             remote(wu_ref, ups.at[core], sib_send.at[1], sib_recv.at[1], other),
             remote(wd_ref, sib_ref, sib_send.at[2], sib_recv.at[2], other)]
    for copy in loads + swaps:
        copy.start()

    def line_of(table, name):
        names = lax.broadcasted_iota(jnp.int32, table.shape, 0)
        return jnp.sum(jnp.where(names == name, table, 0.0), axis=0, keepdims=True)

    def column(flat):
        square = (rows, rows)
        same = lax.broadcasted_iota(jnp.int32, square, 0) == lax.broadcasted_iota(jnp.int32, square, 1)
        return jnp.sum(jnp.where(same, jnp.broadcast_to(flat, square), 0.0), axis=1, keepdims=True)

    def chosen_rows(table, owner):
        slots = jnp.broadcast_to(line_of(table, experts + owner), (cap, rows)).astype(jnp.int32)
        return slots == lax.broadcasted_iota(jnp.int32, (cap, rows), 0)

    def ones(mask):
        return jnp.where(mask, 1.0, 0.0).astype(jnp.bfloat16)

    def spread(table, owner):
        slots = jnp.broadcast_to(column(line_of(table, experts + owner)), (rows, cap)).astype(jnp.int32)
        return ones(slots == lax.broadcasted_iota(jnp.int32, (rows, cap), 1))

    def narrow(mask, source, target):
        def one(t, carry):
            cols = pl.ds(pl.multiple_of(t * units, units), units)
            target[:, cols] = jnp.dot(mask, source[:, cols], preferred_element_type=jnp.float32).astype(jnp.bfloat16)
            return carry

        lax.fori_loop(0, part // units, one, 0)

    def narrow_weight(table):
        picked = chosen_rows(table, me)
        return jnp.sum(jnp.where(picked, jnp.broadcast_to(line_of(table, me), (cap, rows)), 0.0), axis=1, keepdims=True)

    def expand(chunks, weight, target):
        def one(q, carry):
            r, n = q // (units // TILE), q % (units // TILE)
            cols = pl.ds(pl.multiple_of(n * TILE, TILE), TILE)
            gate_act = jnp.zeros((weight.shape[0], TILE), jnp.float32)
            up_act = gate_act
            for j, chunk in enumerate(chunks):
                deep = pl.ds(j * part, part)
                gate_act += jnp.dot(chunk[...], gates[r, deep, cols], preferred_element_type=jnp.float32)
                up_act += jnp.dot(chunk[...], ups[r, deep, cols], preferred_element_type=jnp.float32)
            value = gate_act / (1.0 + jnp.exp(-gate_act)) * up_act * weight
            target[:, pl.ds(pl.multiple_of(q * TILE, TILE), TILE)] = value.astype(jnp.bfloat16)
            return carry

        lax.fori_loop(0, 2 * units // TILE, one, 0)

    for dist in range(1, half):
        for side in range(2):
            tables[dist, side].wait_recv()
            if (dist + 1, side) in tables:
                tables[dist + 1, side].start()
        if dist == half - 1:
            for side in range(2):
                for j in range(SUBS):
                    hops[2, side, j].wait_send()
        for j in range(SUBS):
            for side in range(2):
                hops[dist, side, j].wait_recv()
                if (dist + 1, side, j) not in hops:
                    continue
                if dist + 1 == half or (dist + 1 == half - 1 and j != side):
                    mask = ones(chosen_rows(held_wt[dist - 1, side], ahead[side][1]))
                    narrow(mask, held.at[dist - 1, j, side_rows(side)],
                           stage_far.at[side] if dist + 1 == half else stage.at[side])
                hops[dist + 1, side, j].start()
        if dist == 1:
            for copy in loads:
                copy.wait()
            for copy in swaps[:2]:
                copy.wait()
            expand([own.at[j] for j in range(SUBS)], column(line_of(own_wt[...], me)), hid_own)
        if dist < half - 1:
            weight = jnp.concatenate([column(line_of(held_wt[dist - 1, side], me)) for side in range(2)], axis=0)
            expand([held.at[dist - 1, j] for j in range(SUBS)], weight, hid.at[dist - 1])
        else:
            for side in range(2):
                mask = ones(chosen_rows(held_wt[dist - 1, side], me))
                narrow(mask, held.at[dist - 1, side, side_rows(side)], late.at[side, cap_rows(side)])
            weight = jnp.concatenate([narrow_weight(held_wt[dist - 1, side]) for side in range(2)], axis=0)
            expand([late.at[j] for j in range(SUBS)], weight, hid_late)
    swaps[2].wait()

    back = ((left, right_owner), (right, left_owner))
    sums = {}

    def send(k, side, j, src, dst):
        copy = remote(src, dst, rs_send.at[k, side, j], rs_recv.at[k, side, j], back[side][0])
        copy.start()
        sums[k, side, j] = copy

    per_part = part // units

    def tile_copies(b, slot):
        place = pl.ds(pl.multiple_of(b * units, units), units)
        return [pltpu.make_async_copy(wd_ref.at[:, place], tiles.at[slot, core], tile_sem.at[slot, 0]),
                pltpu.make_async_copy(sib_ref.at[:, place], tiles.at[slot, 1 - core], tile_sem.at[slot, 1])]

    for side in range(2):
        for j in range(SUBS):
            if j != side:
                hops[half - 1, side, j].wait_send()
    for copy in tile_copies(0, 0):
        copy.start()
    for j in range(SUBS):
        def late_one(t, carry, j=j):
            b = j * per_part + t
            slot = b % 2

            @pl.when(b + 1 < SUBS * per_part)
            def _():
                for copy in tile_copies(b + 1, 1 - slot):
                    copy.start()

            for copy in tile_copies(b, slot):
                copy.wait()
            total = jnp.dot(hid_late[cap_rows(j), :units], tiles[slot, 0], preferred_element_type=jnp.float32)
            total += jnp.dot(hid_late[cap_rows(j), units:], tiles[slot, 1], preferred_element_type=jnp.float32)
            stage[j, :, pl.ds(pl.multiple_of(t * units, units), units)] = total.astype(jnp.bfloat16)
            return carry

        lax.fori_loop(0, per_part, late_one, 0)
        send(1, j, j, stage.at[j], late_in.at[j])
    tables[half, 0].wait_recv()
    for side in range(2):
        hops[half, side, side].wait_recv()
    expand([far.at[j] for j in range(SUBS)], narrow_weight(far_wt[...]), hid_far)
    for name, copy in hops.items():
        if name[0] != 2 and not (name[0] == half - 1 and name[1] != name[2]):
            copy.wait_send()
    for copy in tables.values():
        copy.wait_send()

    blocks = width // units

    def down_copy(r, b):
        place = pl.ds(pl.multiple_of(b * units, units), units)
        return [pltpu.make_async_copy(wd_ref.at[:, place], gates.at[core, place], down_sem.at[0, b]),
                pltpu.make_async_copy(sib_ref.at[:, place], gates.at[1 - core, place], down_sem.at[1, b])]

    def start_down(b, carry):
        for copy in down_copy(0, b):
            copy.start()
        return carry

    def wait_down(b, carry):
        for copy in down_copy(0, b):
            copy.wait()
        return carry

    lax.fori_loop(0, blocks, start_down, 0)
    def contract(j, hidden, write):
        def one(t, carry):
            place = pl.ds(pl.multiple_of((j * (part // units) + t) * units, units), units)
            total = jnp.dot(hidden[:, :units], gates[0, place, :], preferred_element_type=jnp.float32)
            total += jnp.dot(hidden[:, units:], gates[1, place, :], preferred_element_type=jnp.float32)
            write(pl.ds(pl.multiple_of(t * units, units), units), total)
            return carry

        lax.fori_loop(0, part // units, one, 0)

    for j in range(SUBS):
        side = 1 - j

        def write(cols, total, side=side):
            stage_far[side, :, cols] = total.astype(jnp.bfloat16)

        lax.fori_loop(j * per_part, (j + 1) * per_part, wait_down, 0)
        contract(j, hid_far, write)
        send(0, side, j, stage_far.at[side], first_in.at[side])
    for j in range(SUBS):
        side = 1 - j
        table = held_wt[half - 2, side]
        theirs = spread(table, back[side][1])
        hid_own_rows = jnp.dot(spread(table, me), hid_late[cap_rows(side), :], preferred_element_type=jnp.float32)
        hid_wide[...] = hid_own_rows.astype(jnp.bfloat16)
        sums[0, side, j].wait_recv()

        def write(cols, total, side=side, theirs=theirs):
            second_out[side, :, cols] = (
                total + jnp.dot(theirs, first_in[side, :, cols], preferred_element_type=jnp.float32)).astype(jnp.bfloat16)

        contract(j, hid_wide, write)
        send(1, side, j, second_out.at[side], held.at[0, j, side_rows(side)])
    for k in range(2, half):
        dist = half - k
        for j in range(SUBS):
            for side in range(2):
                sums[k - 1, side, j].wait_recv()
            if k == 2:
                theirs = spread(held_wt[dist - 1, j], back[j][1])

                def write(cols, total, j=j, theirs=theirs):
                    early, full = slice(j * rows, (j + 1) * rows), slice((1 - j) * rows, (2 - j) * rows)
                    held[0, j, early, cols] = (total[early] + jnp.dot(
                        theirs, late_in[j, :, cols], preferred_element_type=jnp.float32)).astype(jnp.bfloat16)
                    held[0, j, full, cols] = (
                        total[full] + held[0, j, full, cols].astype(jnp.float32)).astype(jnp.bfloat16)
            else:
                def write(cols, total, k=k, j=j):
                    held[k - 2, j, :, cols] = (
                        total + held[k - 2, j, :, cols].astype(jnp.float32)).astype(jnp.bfloat16)

            contract(j, hid.at[dist - 1], write)
            for side in range(2):
                send(k, side, j, held.at[k - 2, j, side_rows(side)], held.at[k - 1, j, side_rows(side)])
    for j in range(SUBS):
        for side in range(2):
            sums[half - 1, side, j].wait_recv()

        def write(cols, total, j=j):
            both = held[half - 2, j, :rows, cols].astype(jnp.float32) + held[half - 2, j, rows:, cols].astype(jnp.float32)
            own[j, :, cols] = (total + both).astype(jnp.bfloat16)

        contract(j, hid_own, write)
        out_ref[:, j * part:(j + 1) * part] = own[j]
    for copy in sums.values():
        copy.wait_send()


def ring_shards(tokens, expert_ids, gate_values, w_gate, w_up, w_down):
    experts = lax.axis_size("expert")
    rows, width = tokens.shape
    units = w_gate.shape[2]
    half = experts // 2
    chosen = expert_ids.T[:, None, :] == jnp.arange(experts, dtype=jnp.int32)[None, :, None]
    weight = jnp.sum(jnp.where(chosen, gate_values.T[:, None, :], 0.0), axis=0)
    named = jnp.any(chosen, axis=0)
    before = (jnp.arange(rows)[:, None] < jnp.arange(rows)[None, :]).astype(jnp.bfloat16)
    slots = jnp.dot(named.astype(jnp.bfloat16), before, preferred_element_type=jnp.float32)
    table = jnp.concatenate([weight, jnp.where(named, slots, -1.0)], axis=0)
    cap = (rows * expert_ids.shape[1] * 5 // (4 * experts) + 15) // 16 * 16
    part = width // SUBS
    bf, f32 = jnp.bfloat16, jnp.float32
    dma = pltpu.SemaphoreType.DMA
    anywhere = pl.BlockSpec(memory_space=pl.ANY)
    out, _ = pl.pallas_call(
        functools.partial(ring_kernel, experts),
        out_shape=(jax.ShapeDtypeStruct((rows, width), bf), jax.ShapeDtypeStruct((units, width), bf)),
        in_specs=[anywhere] * 5,
        out_specs=(pl.BlockSpec(memory_space=pltpu.VMEM), anywhere),
        scratch_shapes=[
            pltpu.VMEM((2, width, units), bf),
            pltpu.VMEM((2, width, units), bf),
            pltpu.VMEM((SUBS, rows, part), bf),
            pltpu.VMEM((half - 1, SUBS, 2 * rows, part), bf),
            pltpu.VMEM((SUBS, 2 * cap, part), bf),
            pltpu.VMEM((SUBS, cap, part), bf),
            pltpu.VMEM((2 * experts, rows), f32),
            pltpu.VMEM((half - 1, 2, 2 * experts, rows), f32),
            pltpu.VMEM((2 * experts, rows), f32),
            pltpu.VMEM((rows, 2 * units), bf),
            pltpu.VMEM((half - 2, 2 * rows, 2 * units), bf),
            pltpu.VMEM((2 * cap, 2 * units), bf),
            pltpu.VMEM((cap, 2 * units), bf),
            pltpu.VMEM((rows, 2 * units), bf),
            pltpu.VMEM((2, cap, part), bf),
            pltpu.VMEM((2, cap, part), bf),
            pltpu.VMEM((2, cap, part), bf),
            pltpu.VMEM((2, cap, part), bf),
            pltpu.VMEM((2, rows, part), bf),
            pltpu.VMEM((2, 2, units, units), bf),
            dma((3 + SUBS,)), dma((3,)), dma((3,)),
            dma((half, 2, SUBS)), dma((half, 2, SUBS)),
            dma((half, 2)), dma((half, 2)),
            dma((half, 2, SUBS)), dma((half, 2, SUBS)),
            dma((2, width // units)), dma((2, 2)),
        ],
        compiler_params=pltpu.CompilerParams(
            collective_id=0, has_side_effects=True, vmem_limit_bytes=60 * 2 ** 20),
    )(tokens, table, w_gate[0], w_up[0], w_down[0])
    return out


def shards(tokens, expert_ids, gate_values, w_gate, w_up, w_down):
    experts = lax.axis_size("expert")
    tok_rows = tokens.shape[0]
    top_count = expert_ids.shape[1]
    width = tokens.shape[1]
    capacity = (tok_rows * top_count * 5 // (4 * experts) + 7) // 8 * 8
    flat_ids = expert_ids.reshape(-1)
    onehot = (flat_ids[:, None] == jnp.arange(experts, dtype=jnp.int32)[None, :]).astype(jnp.int32)
    before = jnp.cumsum(onehot, axis=0) - onehot
    slot_index = jnp.sum(before * onehot, axis=1)
    position = flat_ids * capacity + slot_index
    placing = jnp.arange(experts * capacity, dtype=jnp.int32)[:, None] == position[None, :]
    placing = jnp.sum(
        placing.reshape(experts * capacity, tok_rows, top_count).astype(jnp.int32), axis=2
    ).astype(jnp.bfloat16)
    outgoing = jnp.dot(placing, tokens, preferred_element_type=jnp.float32).astype(jnp.bfloat16)
    outgoing = outgoing.reshape(experts, capacity, width)
    gate_proj = w_gate[0]
    up_proj = w_up[0]
    down_proj = w_down[0]
    paired = lax.all_gather(
        lax.all_to_all(outgoing, "expert", split_axis=0, concat_axis=0, tiled=True),
        "attn",
        axis=1,
        tiled=True,
    )
    flat_rows = paired.reshape(-1, width)
    gate_act = jnp.dot(flat_rows, gate_proj, preferred_element_type=jnp.float32)
    up_act = jnp.dot(flat_rows, up_proj, preferred_element_type=jnp.float32)
    hidden = (jax.nn.silu(gate_act) * up_act).astype(jnp.bfloat16)
    partial_value = (
        jnp.dot(hidden, down_proj, preferred_element_type=jnp.float32)
        .astype(jnp.bfloat16)
        .reshape(paired.shape)
    )
    summed = (
        lax.psum_scatter(partial_value, "attn", scatter_dimension=1, tiled=True)
        .astype(jnp.float32)
        .astype(jnp.bfloat16)
    )
    returned = lax.all_to_all(summed, "expert", split_axis=0, concat_axis=0, tiled=True)
    picked = returned.reshape(experts * capacity, width)[position]
    picked = picked.reshape(tok_rows, top_count, width)
    mixed_out = jnp.sum(picked.astype(jnp.float32) * gate_values[:, :, None], axis=1)
    return mixed_out.astype(jnp.bfloat16)


def solution(mesh):
    placed = (
        P(("group", "expert", "attn"), None),
        P(("group", "expert", "attn"), None),
        P(("group", "expert", "attn"), None),
        P("expert", None, "attn"),
        P("expert", None, "attn"),
        P("expert", "attn", None),
    )

    def run(tokens, expert_ids, gate_values, w_gate, w_up, w_down):
        experts, cores = mesh.shape["expert"], mesh.shape["attn"]
        block = tokens.size * 2 // mesh.size
        weights = w_gate.size * 2 // experts
        need = block * (experts + 7) + 2 * weights
        fits = cores == 2 and experts % 2 == 0 and experts >= 8 and need <= 58 * 2 ** 20
        return jax.shard_map(
            ring_shards if fits else shards,
            mesh=mesh,
            in_specs=placed,
            out_specs=P(("group", "expert", "attn"), None),
            check_vma=False,
        )(tokens, expert_ids, gate_values, w_gate, w_up, w_down)

    return run
```
